256 devices in a mesh: ctx: 32 (over y, x, z_hi), tp: 8 (over z_lo, core).
Axes of the slice: x: 4, y: 4, z: 8 (z_hi: 2, z_lo: 4; z = z_hi * 4 + z_lo), core: 2. Of those that a mesh axis runs over, the one named last changes fastest.
Arguments:
- queries: bfloat16 [4096, 16384], P('ctx', 'tp'), may hold values from -128 to 128
- keys: bfloat16 [4096, 1024], P('ctx', 'tp'), may hold values from -8 to 8
- values: bfloat16 [4096, 1024], P('ctx', 'tp'), may hold values from -6 to 6
- outputs: bfloat16 [4096, 16384], P('ctx', 'tp'), may hold values from -6 to 6
- out_grad: bfloat16 [4096, 16384], P('ctx', 'tp'), may hold values from -8 to 8
- doc_lengths: int32 [8], replicated, may hold values from 1 to 2048, 4096 in all
- span_perm: int32 [64], replicated, may hold values from 0 to 63, each once
Outputs:
- query_grad: bfloat16 [4096, 16384], P('ctx', 'tp')
- key_grad: bfloat16 [4096, 1024], P('ctx', 'tp')
- value_grad: bfloat16 [4096, 1024], P('ctx', 'tp')
- grad_square: float32 [], replicated
The draws below stay inside these ranges and needn't reach their ends.
Inputs may be any that keep to these rules, and one draw needn't show every extreme that they name: `doc_lengths`: the lengths sum to 4096; the longest is exactly 2048. `span_perm`: each span number appears once.
All inputs are finite; a program needn't handle non-finite values.
Results may differ from the reference program's by a relative error of at most 0.0065.
Values may be sent and summed in bfloat16 or wider, within the bound.
No kernel may reach another device: no remote copies, remote signals or barrier semaphores. Data moves between devices by JAX's collectives and lax.ppermute only.
A program may use at most 64 MiB of HBM per device.

```python
import math
import jax
import jax.numpy as jnp
import numpy as np
from jax import lax

HD = 128
GROUP = 16
DOCS = 8
KVH = 8
QH = 128
TOKENS = 4096
SPAN = 64
SPANS = 64


def draw_queries(key, part):
    key = jax.random.fold_in(key, 11)
    result = jnp.clip(jax.random.normal(key, (TOKENS, KVH, GROUP, HD), jnp.float32), -6.0, 6.0)
    return result.reshape(TOKENS, KVH * GROUP * HD).astype(jnp.bfloat16)


def draw_keys(key, part):
    key = jax.random.fold_in(key, 12)
    result = jnp.clip(jax.random.normal(key, (TOKENS, KVH, HD), jnp.float32), -6.0, 6.0)
    return result.reshape(TOKENS, KVH * HD).astype(jnp.bfloat16)


def draw_out_grad(key, part):
    key = jax.random.fold_in(key, 13)
    column_key = jax.random.fold_in(key, 1)
    entry_key = jax.random.fold_in(key, 2)
    column_base = jnp.clip(jax.random.normal(column_key, (QH * HD,), jnp.float32), -3.0, 3.0)
    offset = 0.5 * column_base
    noise = jnp.clip(jax.random.normal(entry_key, (TOKENS, QH * HD), jnp.float32), -6.0, 6.0)
    return (noise + offset[None, :]).astype(jnp.bfloat16)


def steps_of(stream_key, dims, shards, smallest, top_value):
    gain = 1.0
    for dim, shards_of in shards:
        steps = jax.random.uniform(jax.random.fold_in(jax.random.fold_in(stream_key, 6), dim), (shards_of,), jnp.float32, smallest / len(shards), top_value / len(shards))
        gain = gain * jnp.repeat(jnp.exp(steps), dims[dim] // shards_of).reshape((-1,) + (1,) * (len(dims) - 1 - dim))
    return gain


def length_profile(amount, total, bound, lean):
    weights = [(1 << 20) // math.isqrt(rank ** lean) + 1 for rank in range(2, amount + 1)]
    surplus, given = total - bound - (amount - 1), [1] * (amount - 1)
    while surplus > 0:
        free = [i for i in range(amount - 1) if given[i] < bound]
        pool, left = sum([weights[i] for i in free]), surplus
        for i in free:
            extra = min(bound - given[i], max(1, left * weights[i] // pool), surplus)
            given[i] = given[i] + extra
            surplus = surplus - extra
    return np.array([bound] + given)


def uneven_parts(key, amount, total, limit, slope):
    if amount == 2:
        one = jax.random.randint(key, (), max(1, total - limit), min(limit, total - 1) + 1)
        return jnp.stack([one, total - one])
    sizes = jnp.asarray(length_profile(amount, total, limit, slope), jnp.int32)
    pairs = (amount - 1) // 2
    donor, receiver = sizes[1:1 + 2 * pairs:2], sizes[2:2 + 2 * pairs:2]
    margin = jnp.minimum(donor - 1, limit - receiver)
    moved = jax.random.randint(jax.random.fold_in(key, 1), (pairs,), 0, 1 << 20) % (margin + 1)
    sizes = sizes.at[1:1 + 2 * pairs:2].set(donor - moved).at[2:2 + 2 * pairs:2].set(receiver + moved)
    return sizes[jax.random.permutation(jax.random.fold_in(key, 2), amount)]


def gaussian(stream_key, shape, width, reach, split=(), held_as=jnp.bfloat16):
    gain = steps_of(stream_key, shape, split, -0.22, 0.18) if split else 1.0
    values = jax.random.normal(stream_key, shape, jnp.float32) * width * gain
    return jnp.minimum(jnp.maximum(values, -reach), reach).astype(held_as)


def setup_inputs(seed: int = 0) -> dict:
    key_list = jax.random.split(jax.random.key(seed), 8)
    queries = draw_queries(jax.random.fold_in(key_list[7], 71), 0)
    keys = draw_keys(jax.random.fold_in(key_list[7], 71), 0)
    values = gaussian(key_list[2], (TOKENS, KVH * HD), 1.0, 6.0, ((0, 32), (1, 8)))
    outputs = gaussian(key_list[3], (TOKENS, QH * HD), 1.0, 6.0, ((0, 32), (1, 8)))
    out_grad = draw_out_grad(jax.random.fold_in(key_list[7], 71), 0)
    doc_lengths = uneven_parts(key_list[5], DOCS, TOKENS, TOKENS // 2, 2).astype(jnp.int32)
    span_perm = jax.random.permutation(key_list[6], SPANS).astype(jnp.int32)
    return {"queries": queries, "keys": keys, "values": values, "outputs": outputs, "out_grad": out_grad, "doc_lengths": doc_lengths, "span_perm": span_perm}


def layout_places(span_perm, count, span):
    rows = jnp.arange(count, dtype=jnp.int32)
    return span_perm[rows // span].astype(jnp.int32) * span + rows % span


def reference(queries, keys, values, outputs, out_grad, doc_lengths, span_perm):
    scale = HD ** -0.5
    places = layout_places(span_perm, TOKENS, SPAN)
    ends = jnp.cumsum(doc_lengths)
    docs = jnp.sum((places[:, None] >= ends[None, :]).astype(jnp.int32), axis=1)
    allowed = (places[None, :] <= places[:, None]) & (docs[None, :] == docs[:, None])
    query_heads = queries.reshape(TOKENS, KVH, GROUP, HD).transpose(1, 2, 0, 3)
    grad_heads = out_grad.reshape(TOKENS, KVH, GROUP, HD).transpose(1, 2, 0, 3)
    out_heads = outputs.reshape(TOKENS, KVH, GROUP, HD).transpose(1, 2, 0, 3)
    key_heads = keys.reshape(TOKENS, KVH, HD).transpose(1, 0, 2)
    value_heads = values.reshape(TOKENS, KVH, HD).transpose(1, 0, 2)

    def one_group(packed):
        qgroup, dgroup, ogroup, kgroup, vgroup = packed

        def one_head(carry, head):
            qh, dh, oh = head
            scores = jnp.dot(qh, kgroup.T, preferred_element_type=jnp.float32) * scale
            high = jnp.max(jnp.where(allowed, scores, -jnp.inf), axis=1, keepdims=True)
            total = jnp.sum(jnp.where(allowed, jnp.exp(scores - high), 0.0), axis=1, keepdims=True)
            lse = high + jnp.log(total)
            probs = jnp.where(allowed, jnp.exp(scores - lse), 0.0)
            dprobs = jnp.dot(dh, vgroup.T, preferred_element_type=jnp.float32)
            delta = jnp.sum(dh.astype(jnp.float32) * oh.astype(jnp.float32), axis=1, keepdims=True)
            dscores = (probs * (dprobs - delta)).astype(jnp.bfloat16)
            query_part = jnp.dot(dscores, kgroup, preferred_element_type=jnp.float32) * scale
            key_part = jnp.dot(dscores.T, qh, preferred_element_type=jnp.float32) * scale
            value_part = jnp.dot(probs.astype(jnp.bfloat16).T, dh, preferred_element_type=jnp.float32)
            return (carry[0] + key_part, carry[1] + value_part), query_part.astype(jnp.bfloat16)

        start = (jnp.zeros((TOKENS, HD), jnp.float32), jnp.zeros((TOKENS, HD), jnp.float32))
        sums, query_parts = lax.scan(one_head, start, (qgroup, dgroup, ogroup))
        return query_parts, sums[0].astype(jnp.bfloat16), sums[1].astype(jnp.bfloat16)

    query_parts, key_parts, value_parts = lax.map(one_group, (query_heads, grad_heads, out_heads, key_heads, value_heads))
    query_grad = query_parts.transpose(2, 0, 1, 3).reshape(TOKENS, QH * HD)
    key_grad = key_parts.transpose(1, 0, 2).reshape(TOKENS, KVH * HD)
    value_grad = value_parts.transpose(1, 0, 2).reshape(TOKENS, KVH * HD)
    grad_square = (jnp.sum(jnp.square(query_grad.astype(jnp.float32))) + jnp.sum(jnp.square(key_grad.astype(jnp.float32))) + jnp.sum(jnp.square(value_grad.astype(jnp.float32))))
    return query_grad, key_grad, value_grad, grad_square
```

```python
import functools

import jax
import jax.numpy as jnp
from jax import lax
from jax.experimental import pallas as pl
from jax.experimental.pallas import tpu as pltpu
from jax.sharding import PartitionSpec as P

HD = 128
GROUP = 16
SPAN = 64
SPANS = 64
NY, NX, NZ = 4, 4, 2
ROWS = SPAN * GROUP
TILE = 256
TOTAL = SPAN * SPANS
SCALE = HD ** (-0.5)
LOG2E = 1.4426950408889634
NEG = -1e30

f32, bf16, i32 = jnp.float32, jnp.bfloat16, jnp.int32


def nt(a, b):
    return lax.dot_general(a, b, (((1,), (1,)), ((), ())), preferred_element_type=f32)


def nn(a, b):
    return lax.dot_general(a, b, (((1,), (0,)), ((), ())), preferred_element_type=f32)


def tn(a, b):
    return lax.dot_general(a, b, (((0,), (0,)), ((), ())), preferred_element_type=f32)


def rel_slots():
    return [
        (sy, sx, sz, half)
        for sy in range(NY)
        for sx in range(NX)
        for sz in range(NZ)
        for half in range(2)
    ]


def attention_kernel(
    perm_ref, lens_ref, q_ref, o_ref, g_ref, kv0, kv1, kv2, kv3,
    dq_ref, d0, d1, d2, d3, sq_ref,
    qs, gs, kseq, vseq, acc, dqt,
):
    kvs, outs = (kv0, kv1, kv2, kv3), (d0, d1, d2, d3)
    me = lax.axis_index("ctx")
    y, x, z = me // (NX * NZ), (me // NZ) % NX, me % NZ

    def span_of(sy, sx, sz, half):
        slot = ((((y + NY - sy) % NY) * NX + (x + NX - sx) % NX) * NZ + (z + sz) % NZ) * 2 + half
        return perm_ref[slot]

    for a in range(2):
        for h in range(GROUP):
            dst = pl.ds(a * ROWS + h * SPAN, SPAN)
            src = (pl.ds(a * SPAN, SPAN), pl.ds(h * HD, HD))
            qs[dst, :] = q_ref[src]
            gs[dst, :] = g_ref[src]

    for i, (sy, sx, sz, half) in enumerate(rel_slots()):
        at = pl.multiple_of(span_of(sy, sx, sz, half) * SPAN, SPAN)
        row = (i * SPAN) % (TOTAL // NY)
        kseq[pl.ds(at, SPAN), :] = kvs[sy][pl.ds(row, SPAN), :HD]
        vseq[pl.ds(at, SPAN), :] = kvs[sy][pl.ds(row, SPAN), HD:]
    kseq[pl.ds(TOTAL, TILE), :] = jnp.zeros((TILE, HD), bf16)
    vseq[pl.ds(TOTAL, TILE), :] = jnp.zeros((TILE, HD), bf16)
    acc[...] = jnp.zeros_like(acc)

    ends, total = [], 0
    for d in range(lens_ref.shape[0]):
        total = total + lens_ref[d]
        ends.append(total)

    lane = lax.broadcasted_iota(i32, (1, ROWS), 1)
    square = jnp.zeros((1, 1), f32)
    for a in range(2):
        span = perm_ref[me * 2 + a]
        place = span * SPAN + (lane & (SPAN - 1))
        begin = jnp.zeros_like(place)
        first = 0
        for end in ends:
            begin = jnp.maximum(begin, jnp.where(end <= place, end, 0))
            first = jnp.maximum(first, jnp.where(end <= span * SPAN, end, 0))
        start = (first // SPAN) * SPAN
        count = (span * SPAN + SPAN - start + TILE - 1) // TILE
        q = qs[pl.ds(a * ROWS, ROWS), :]
        g = gs[pl.ds(a * ROWS, ROWS), :]

        prods = []
        for h in range(GROUP):
            src = (pl.ds(a * SPAN, SPAN), pl.ds(h * HD, HD))
            prods.append(g_ref[src].astype(f32) * o_ref[src].astype(f32))
        prod = jnp.concatenate(prods, axis=0)
        high = prod.astype(bf16)
        low = (prod - high.astype(f32)).astype(bf16)
        ones = jnp.ones((16, HD), bf16)
        delta = (nt(ones, high) + nt(ones, low))[:1]

        def visible(k0):
            kp = k0 + lax.broadcasted_iota(i32, (TILE, 1), 0)
            return (kp <= place) & (kp >= begin)

        def stats(t, state):
            peak, mass = state
            k0 = pl.multiple_of(start + t * TILE, SPAN)
            s = nt(kseq[pl.ds(k0, TILE), :], q) * (SCALE * LOG2E)
            s = jnp.where(visible(k0), s, NEG)
            fresh = jnp.maximum(peak, jnp.max(s, axis=0, keepdims=True))
            part = jnp.sum(jnp.exp2(s - fresh), axis=0, keepdims=True)
            return fresh, mass * jnp.exp2(peak - fresh) + part

        peak, mass = lax.fori_loop(
            0, count, stats, (jnp.full((1, ROWS), NEG, f32), jnp.zeros((1, ROWS), f32))
        )
        lse = peak + jnp.log2(mass)

        dqt[...] = jnp.zeros_like(dqt)

        def grads(t, carry):
            k0 = pl.multiple_of(start + t * TILE, SPAN)
            k = kseq[pl.ds(k0, TILE), :]
            v = vseq[pl.ds(k0, TILE), :]
            s = nt(k, q) * (SCALE * LOG2E)
            p = jnp.where(visible(k0), jnp.exp2(s - lse), 0.0)
            ds = (p * (nt(v, g) - delta)).astype(bf16)
            acc[pl.ds(k0, TILE), :HD] += nn(ds, q)
            acc[pl.ds(k0, TILE), HD:] += nn(p.astype(bf16), g)
            dqt[...] += tn(k, ds)
            return carry

        lax.fori_loop(0, count, grads, 0)
        dq = (dqt[...] * SCALE).T.astype(bf16)
        for h in range(GROUP):
            dq_ref[pl.ds(a * SPAN, SPAN), pl.ds(h * HD, HD)] = dq[h * SPAN : (h + 1) * SPAN]
        dq = dq.astype(f32)
        square = square + jnp.sum(jnp.sum(dq * dq, axis=0, keepdims=True), axis=1, keepdims=True)

    sq_ref[...] = jnp.broadcast_to(square, sq_ref.shape)
    for i, (sy, sx, sz, half) in enumerate(rel_slots()):
        at = pl.multiple_of(span_of(sy, sx, sz, half) * SPAN, SPAN)
        row = (i * SPAN) % (TOTAL // NY)
        outs[sy][pl.ds(row, SPAN), :HD] = (acc[pl.ds(at, SPAN), :HD] * SCALE).astype(bf16)
        outs[sy][pl.ds(row, SPAN), HD:] = acc[pl.ds(at, SPAN), HD:].astype(bf16)


def attention(span_perm, doc_lengths, queries, outputs, out_grad, kvs):
    tq = queries.shape[0]
    vm = pl.BlockSpec(memory_space=pltpu.VMEM)
    sm = pl.BlockSpec(memory_space=pltpu.SMEM)
    chunk = jax.ShapeDtypeStruct((TOTAL // NY, 2 * HD), bf16)
    return pl.pallas_call(
        attention_kernel,
        out_shape=(
            jax.ShapeDtypeStruct(queries.shape, bf16),
            chunk, chunk, chunk, chunk,
            jax.ShapeDtypeStruct((8, HD), f32),
        ),
        in_specs=[sm, sm] + [vm] * 7,
        out_specs=(vm,) * 6,
        scratch_shapes=[
            pltpu.VMEM((2 * ROWS, HD), bf16),
            pltpu.VMEM((2 * ROWS, HD), bf16),
            pltpu.VMEM((TOTAL + TILE, HD), bf16),
            pltpu.VMEM((TOTAL + TILE, HD), bf16),
            pltpu.VMEM((TOTAL + TILE, 2 * HD), f32),
            pltpu.VMEM((HD, ROWS), f32),
        ],
        compiler_params=pltpu.CompilerParams(vmem_limit_bytes=48 * 1024 * 1024),
    )(span_perm, doc_lengths, queries, outputs, out_grad, *kvs)


def moved(a, dy=0, dx=0, dz=0):
    pairs = []
    for y in range(NY):
        for x in range(NX):
            for z in range(NZ):
                to = (((y + dy) % NY) * NX + (x + dx) % NX) * NZ + (z + dz) % NZ
                pairs.append(((y * NX + x) * NZ + z, to))
    return lax.ppermute(a, "ctx", pairs)


def shards(queries, keys, values, outputs, out_grad, doc_lengths, span_perm):
    tq = queries.shape[0]
    kv = jnp.concatenate([keys, values], axis=1)
    kv = jnp.stack([kv, moved(kv, dz=1)])
    kv = jnp.stack([kv] + [moved(kv, dx=s) for s in range(1, NX)])
    kvs = [kv] + [moved(kv, dy=s) for s in range(1, NY)]
    kvs = [a.reshape(TOTAL // NY, 2 * HD) for a in kvs]
    query_grad, *parts, square = attention(
        span_perm, doc_lengths, queries, outputs, out_grad, kvs
    )
    parts = [parts[0]] + [moved(parts[s], dy=-s) for s in range(1, NY)]
    mine = sum(p.astype(f32) for p in parts).astype(bf16).reshape(NX, NZ, tq, 2 * HD)
    parts = [mine[0]] + [moved(mine[s], dx=-s) for s in range(1, NX)]
    mine = sum(p.astype(f32) for p in parts)
    other = moved(mine[1].astype(bf16), dz=1)
    both = (mine[0] + other.astype(f32)).astype(bf16)
    wide = both.astype(f32)
    local = jnp.sum(wide * wide) + square[0, 0]
    world = lax.axis_size(("ctx", "tp"))
    grad_square = jnp.sum(
        lax.all_to_all(jnp.broadcast_to(local, (world, 1)), ("ctx", "tp"), 0, 0)
    )
    return (query_grad, both[:, :HD], both[:, HD:], grad_square)


def solution(mesh):
    placed = (P("ctx", "tp"),) * 5 + (P(), P())
    return jax.shard_map(
        shards,
        mesh=mesh,
        in_specs=placed,
        out_specs=(P("ctx", "tp"), P("ctx", "tp"), P("ctx", "tp"), P()),
        check_vma=False,
    )
```

```python
import jax
import jax.numpy as jnp
from jax import lax
from jax.experimental import pallas as pl
from jax.experimental.pallas import tpu as pltpu
from jax.sharding import Mesh
from jax.sharding import PartitionSpec as P

HD = 128
GROUP = 16
SPAN = 64
SPANS = 64
NY, NX, NZ = 4, 4, 2
ROWS = SPAN * GROUP
TILE = 512
TOTAL = SPAN * SPANS
SCALE = HD ** (-0.5)
LOG2E = 1.4426950408889634
NEG = -1e30
VMEM = 36 * 1024 * 1024

f32, bf16, i32 = jnp.float32, jnp.bfloat16, jnp.int32


def nt(a, b):
    return lax.dot_general(a, b, (((1,), (1,)), ((), ())), preferred_element_type=f32)


def nn(a, b):
    return lax.dot_general(a, b, (((1,), (0,)), ((), ())), preferred_element_type=f32)


def tn(a, b):
    return lax.dot_general(a, b, (((0,), (0,)), ((), ())), preferred_element_type=f32)


def position():
    y, x, z = lax.axis_index("y"), lax.axis_index("x"), lax.axis_index("zh")
    return y, x, z, (y * NX + x) * NZ + z


def slot_place(meta_ref, slot):
    return pl.multiple_of(meta_ref[slot] * SPAN, SPAN)


def each_query_span(meta_ref, body):
    me = position()[3]
    ends, total = [], 0
    for d in range(meta_ref.shape[0] - SPANS):
        total = total + meta_ref[SPANS + d]
        ends.append(total)
    lane = lax.broadcasted_iota(i32, (1, ROWS), 1)
    for a in range(2):
        span = meta_ref[me * 2 + a]
        place = span * SPAN + (lane & (SPAN - 1))
        begin = jnp.zeros_like(place)
        first, last = 0, 0
        for end in ends:
            begin = jnp.maximum(begin, jnp.where(end <= place, end, 0))
            first = jnp.maximum(first, jnp.where(end <= span * SPAN, end, 0))
            last = jnp.maximum(last, jnp.where(end <= span * SPAN + SPAN - 1, end, 0))
        start = (first // SPAN) * SPAN
        count = (span * SPAN + SPAN - start + TILE - 1) // TILE

        def visible(k0, c, n, place=place, begin=begin):
            kp = k0 + lax.broadcasted_iota(i32, (TILE, 1), 0)
            return (kp <= place[:, c : c + n]) & (kp >= begin[:, c : c + n])

        def tiles(step, masked=True, start=start, count=count, span=span, last=last):
            def one(t, carry):
                k0 = pl.multiple_of(start + t * TILE, SPAN)
                whole = (k0 >= last) & (k0 + TILE <= span * SPAN + 1)
                if not masked:
                    step(t, k0, None)
                    return carry

                @pl.when(whole)
                def _():
                    step(t, k0, lambda a, b, c=0, n=ROWS: a)

                @pl.when(jnp.logical_not(whole))
                def _():
                    step(t, k0, lambda a, b, c=0, n=ROWS: jnp.where(visible(k0, c, n), a, b))

                return carry

            lax.fori_loop(0, count, one, 0)

        body(a, pl.ds(a * ROWS, ROWS), tiles)


def sorted_blocks(meta_ref, ks, vs, kseq, vseq):
    y, x, z, _ = position()
    for sy in range(NY):
        for sx in range(NX):
            for zz in range(NZ * 2):
                home = ((y + NY - sy) % NY) * NX + (x + NX - sx) % NX
                at = slot_place(meta_ref, (home * NZ + (z + zz // 2) % NZ) * 2 + zz % 2)
                kseq[pl.ds(at, SPAN), :] = ks[sy][pl.ds((sx * 2 * NZ + zz) * SPAN, SPAN), :]
                vseq[pl.ds(at, SPAN), :] = vs[sx][pl.ds((sy * 2 * NZ + zz) * SPAN, SPAN), :]
    kseq[pl.ds(TOTAL, TILE), :] = jnp.zeros((TILE, HD), bf16)
    vseq[pl.ds(TOTAL, TILE), :] = jnp.zeros((TILE, HD), bf16)


def prepare_kernel(q_ref, o_ref, g_ref, qs, gs, qt, gt, delta):
    for a in range(2):
        prods = []
        for h in range(GROUP):
            dst = pl.ds(a * ROWS + h * SPAN, SPAN)
            src = (pl.ds(a * SPAN, SPAN), pl.ds(h * HD, HD))
            qs[dst, :] = q_ref[src]
            gs[dst, :] = g_ref[src]
            prods.append(g_ref[src].astype(f32) * o_ref[src].astype(f32))
        rows = pl.ds(a * ROWS, ROWS)
        qt[:, rows] = qs[rows, :].T
        gt[:, rows] = gs[rows, :].T
        prod = jnp.concatenate(prods, axis=0)
        high = prod.astype(bf16)
        low = (prod - high.astype(f32)).astype(bf16)
        ones = jnp.ones((16, HD), bf16)
        delta[pl.ds(a * 8, 8), :] = (nt(ones, high) + nt(ones, low))[:8]


def key_value_kernel(
    meta_ref, qs, gs, qt, gt, delta_ref, k0, k1, k2, k3, v0, v1, v2, v3,
    dkv_ref, lse_ref, kseq, vseq, acc, weights, peaks, peak, mass,
):
    sorted_blocks(meta_ref, (k0, k1, k2, k3), (v0, v1, v2, v3), kseq, vseq)
    acc[...] = jnp.zeros_like(acc)

    def span(a, rows, tiles):
        peak[...] = jnp.full_like(peak, NEG)
        mass[...] = jnp.zeros_like(mass)

        def stats(t, at, pick):
            k = kseq[pl.ds(at, TILE), :]
            for c in range(0, ROWS, 256):
                cols = pl.ds(c, 256)
                s = pick(nn(k, qt[:, pl.ds(a * ROWS + c, 256)]), NEG, c, 256)
                old = peak[:, cols]
                fresh = jnp.maximum(old, jnp.max(s, axis=0, keepdims=True))
                e = jnp.exp2(s * (SCALE * LOG2E) - fresh * (SCALE * LOG2E))
                mass[:, cols] = mass[:, cols] * jnp.exp2((old - fresh) * (SCALE * LOG2E)) + jnp.sum(
                    e, axis=0, keepdims=True
                )
                peak[:, cols] = fresh
                peaks[t, :, cols] = jnp.broadcast_to(fresh, (8, 256))
                weights[t, :, cols] = e

        tiles(stats)
        lse = peak[...] * (SCALE * LOG2E) + jnp.log2(mass[...])
        lse_ref[pl.ds(a * 8, 8), :] = jnp.broadcast_to(lse, (8, ROWS))
        delta, high, inverse = delta_ref[pl.ds(a * 8, 1), :], peak[...], 1.0 / mass[...]

        def step(t, at, pick):
            v = vseq[pl.ds(at, TILE), :]
            dk, dv = acc[pl.ds(at, TILE), :HD], acc[pl.ds(at, TILE), HD:]
            for c in range(0, ROWS, 256):
                cols, some = pl.ds(c, 256), pl.ds(a * ROWS + c, 256)
                w = jnp.exp2((peaks[t, :, cols][:1] - high[:, c : c + 256]) * (SCALE * LOG2E)) * inverse[:, c : c + 256]
                p = weights[t, :, cols] * w
                ds = p * (nn(v, gt[:, some]) - delta[:, c : c + 256])
                dv = dv + nn(p.astype(bf16), gs[some, :])
                dk = dk + nn(ds.astype(bf16), qs[some, :])
            acc[pl.ds(at, TILE), :HD] = dk
            acc[pl.ds(at, TILE), HD:] = dv

        tiles(step, masked=False)

    each_query_span(meta_ref, span)
    for slot in range(SPANS):
        at = slot_place(meta_ref, slot)
        row = pl.ds(slot * SPAN, SPAN)
        dkv_ref[row, :HD] = (acc[pl.ds(at, SPAN), :HD] * SCALE).astype(bf16)
        dkv_ref[row, HD:] = acc[pl.ds(at, SPAN), HD:].astype(bf16)


def query_kernel(
    meta_ref, qt, gt, delta_ref, lse_ref, k0, k1, k2, k3, v0, v1, v2, v3,
    dq_ref, sq_ref, kseq, vseq, acc,
):
    sorted_blocks(meta_ref, (k0, k1, k2, k3), (v0, v1, v2, v3), kseq, vseq)
    square = []

    def span(a, rows, tiles):
        lse, delta = lse_ref[pl.ds(a * 8, 1), :], delta_ref[pl.ds(a * 8, 1), :]
        acc[...] = jnp.zeros_like(acc)

        def step(t, at, pick):
            k = kseq[pl.ds(at, TILE), :]
            p = pick(jnp.exp2(nn(k, qt[:, rows]) * (SCALE * LOG2E) - lse), 0.0)
            ds = p * (nn(vseq[pl.ds(at, TILE), :], gt[:, rows]) - delta)
            acc[...] += tn(k, ds.astype(bf16))

        tiles(step)
        dq = (acc[...] * SCALE).T.astype(bf16)
        for h in range(GROUP):
            dq_ref[pl.ds(a * SPAN, SPAN), pl.ds(h * HD, HD)] = dq[h * SPAN : (h + 1) * SPAN]
        dq = dq.astype(f32)
        square.append(jnp.sum(jnp.sum(dq * dq, axis=0, keepdims=True), axis=1, keepdims=True))

    each_query_span(meta_ref, span)
    sq_ref[...] = jnp.broadcast_to(square[0] + square[1], sq_ref.shape)


def call(kernel, outs, smem, scratch, flops, *args):
    vm = pl.BlockSpec(memory_space=pltpu.VMEM)
    sm = pl.BlockSpec(memory_space=pltpu.SMEM)
    return pl.pallas_call(
        kernel,
        out_shape=tuple(jax.ShapeDtypeStruct(s, t) for s, t in outs),
        in_specs=[sm] * smem + [vm] * (len(args) - smem),
        out_specs=(vm,) * len(outs),
        scratch_shapes=[pltpu.VMEM(s, t) for s, t in scratch],
        compiler_params=pltpu.CompilerParams(vmem_limit_bytes=VMEM),
        cost_estimate=pl.CostEstimate(flops=flops, bytes_accessed=4 << 20, transcendentals=0),
    )(*args)


def shift(a, axis, step):
    n = lax.axis_size(axis)
    return lax.ppermute(a, axis, [(i, (i + step) % n) for i in range(n)])


def shards(queries, keys, values, outputs, out_grad, doc_lengths, span_perm):
    tq = queries.shape[0]
    k = jnp.stack([keys, shift(keys, "zh", 1)])
    v = jnp.stack([values, shift(values, "zh", 1)])
    k = [k] + [shift(k, "x", s) for s in range(1, NX)]
    v = [v] + [shift(v, "y", s) for s in range(1, NY)]
    k, v = lax.optimization_barrier((k, v))
    k, v = jnp.stack(k), jnp.stack(v)
    k = [k] + [shift(k, "y", s) for s in range(1, NY)]
    v = [v] + [shift(v, "x", s) for s in range(1, NX)]
    k = [a.reshape(TOTAL // NY, HD) for a in k]
    v = [a.reshape(TOTAL // NX, HD) for a in v]

    meta = jnp.concatenate([span_perm, doc_lengths])
    heads, turned = ((2 * ROWS, HD), bf16), ((HD, 2 * ROWS), bf16)
    row, one, longer = ((16, ROWS), f32), ((1, ROWS), f32), ((TOTAL + TILE, HD), bf16)
    most = -(-(TOTAL // 2 + SPAN) // TILE)
    qs, gs, qt, gt, delta = call(
        prepare_kernel,
        [heads, heads, turned, turned, row],
        0, [], 1 << 30, queries, outputs, out_grad,
    )
    parts, lse = call(
        key_value_kernel,
        [((TOTAL, 2 * HD), bf16), row],
        1,
        [
            longer, longer,
            ((TOTAL + TILE, 2 * HD), f32),
            ((most, TILE, ROWS), f32),
            ((most, 8, ROWS), f32),
            one, one,
        ],
        16 << 30,
        meta, qs, gs, qt, gt, delta, *k, *v,
    )
    parts = parts.reshape(NY * NX, NZ, tq, 2 * HD)
    parts = lax.all_to_all(parts, ("y", "x"), 0, 0)
    query_grad, square = call(
        query_kernel,
        [(queries.shape, bf16), ((8, HD), f32)],
        1,
        [longer, longer, ((HD, ROWS), f32)],
        16 << 30,
        meta, qt, gt, delta, lse, *k, *v,
    )
    parts, query_grad, square = lax.optimization_barrier((parts, query_grad, square))
    z = lax.axis_index("zh")

    def total(index):
        part = lax.dynamic_index_in_dim(parts, index, 1, False)
        return jnp.sum(part.astype(f32), axis=0)

    other = shift(total(1 - z).astype(bf16), "zh", 1)
    both = (total(z) + other.astype(f32)).astype(bf16)
    wide = both.astype(f32)
    local = jnp.sum(wide * wide) + square[0, 0]
    every = ("y", "x", "zh", "tp")
    world = lax.axis_size(every)
    grad_square = jnp.sum(lax.all_to_all(jnp.broadcast_to(local, (world, 1)), every, 0, 0))
    return (query_grad, both[:, :HD], both[:, HD:], grad_square)


def solution(mesh):
    tp = mesh.devices.shape[1]
    split = Mesh(mesh.devices.reshape(NY, NX, NZ, tp), ("y", "x", "zh", "tp"))
    both = P(("y", "x", "zh"), "tp")
    return jax.shard_map(
        shards,
        mesh=split,
        in_specs=(both,) * 5 + (P(), P()),
        out_specs=(both, both, both, P()),
        check_vma=False,
    )
```

```python
import jax
import jax.numpy as jnp
from jax import lax
from jax.experimental import pallas as pl
from jax.experimental.pallas import tpu as pltpu
from jax.sharding import Mesh
from jax.sharding import PartitionSpec as P

HD = 128
GROUP = 16
SPAN = 64
SPANS = 64
NY, NX, NZ = 4, 4, 2
ROWS = SPAN * GROUP
TILE = 512
TOTAL = SPAN * SPANS
SCALE = HD ** (-0.5)
LOG2E = 1.4426950408889634
NEG = -1e30
VMEM = 16 * 1024 * 1024

f32, bf16, i32 = jnp.float32, jnp.bfloat16, jnp.int32


def nt(a, b):
    return lax.dot_general(a, b, (((1,), (1,)), ((), ())), preferred_element_type=f32)


def nn(a, b):
    return lax.dot_general(a, b, (((1,), (0,)), ((), ())), preferred_element_type=f32)


def tn(a, b):
    return lax.dot_general(a, b, (((0,), (0,)), ((), ())), preferred_element_type=f32)


def position():
    y, x, z = lax.axis_index("y"), lax.axis_index("x"), lax.axis_index("zh")
    return y, x, z, (y * NX + x) * NZ + z


def slot_place(meta_ref, slot):
    return pl.multiple_of(meta_ref[slot] * SPAN, SPAN)


def each_query_span(meta_ref, body):
    me = position()[3]
    ends, total = [], 0
    for d in range(meta_ref.shape[0] - SPANS):
        total = total + meta_ref[SPANS + d]
        ends.append(total)
    lane = lax.broadcasted_iota(i32, (1, ROWS), 1)
    for a in range(2):
        span = meta_ref[me * 2 + a]
        place = span * SPAN + (lane & (SPAN - 1))
        begin = jnp.zeros_like(place)
        first, last = 0, 0
        for end in ends:
            begin = jnp.maximum(begin, jnp.where(end <= place, end, 0))
            first = jnp.maximum(first, jnp.where(end <= span * SPAN, end, 0))
            last = jnp.maximum(last, jnp.where(end <= span * SPAN + SPAN - 1, end, 0))
        start = (first // SPAN) * SPAN
        count = (span * SPAN + SPAN - start + TILE - 1) // TILE

        def visible(k0, c, n, place=place, begin=begin):
            kp = k0 + lax.broadcasted_iota(i32, (TILE, 1), 0)
            return (kp <= place[:, c : c + n]) & (kp >= begin[:, c : c + n])

        def tiles(step, masked=True, start=start, count=count, span=span, last=last):
            def one(t, carry):
                k0 = pl.multiple_of(start + t * TILE, SPAN)
                whole = (k0 >= last) & (k0 + TILE <= span * SPAN + 1)
                if not masked:
                    step(t, k0, None)
                    return carry

                @pl.when(whole)
                def _():
                    step(t, k0, lambda a, b, c=0, n=ROWS: a)

                @pl.when(jnp.logical_not(whole))
                def _():
                    step(t, k0, lambda a, b, c=0, n=ROWS: jnp.where(visible(k0, c, n), a, b))

                return carry

            lax.fori_loop(0, count, one, 0)

        body(a, pl.ds(a * ROWS, ROWS), tiles)


def sorted_blocks(meta_ref, pieces, seq, keys):
    y, x, z, _ = position()
    for sy in range(NY):
        for sx in range(NX):
            for zz in range(NZ * 2):
                home = ((y + NY - sy) % NY) * NX + (x + NX - sx) % NX
                at = slot_place(meta_ref, (home * NZ + (z + zz // 2) % NZ) * 2 + zz % 2)
                last, inner = (sy, sx) if keys else (sx, sy)
                row = pl.ds((inner * 2 * NZ + zz) * SPAN, SPAN)
                seq[pl.ds(at, SPAN), :] = pieces[last][row, :]
    seq[pl.ds(TOTAL, TILE), :] = jnp.zeros((TILE, HD), bf16)


def prepare_kernel(q_ref, o_ref, g_ref, qs, gs, qt, gt, delta):
    for a in range(2):
        prods = []
        for h in range(GROUP):
            dst = pl.ds(a * ROWS + h * SPAN, SPAN)
            src = (pl.ds(a * SPAN, SPAN), pl.ds(h * HD, HD))
            qs[dst, :] = q_ref[src]
            gs[dst, :] = g_ref[src]
            prods.append(g_ref[src].astype(f32) * o_ref[src].astype(f32))
        rows = pl.ds(a * ROWS, ROWS)
        qt[:, rows] = qs[rows, :].T
        gt[:, rows] = gs[rows, :].T
        prod = jnp.concatenate(prods, axis=0)
        high = prod.astype(bf16)
        low = (prod - high.astype(f32)).astype(bf16)
        ones = jnp.ones((16, HD), bf16)
        delta[pl.ds(a * 8, 8), :] = (nt(ones, high) + nt(ones, low))[:8]


def score_kernel(
    meta_ref, qt, k0, k1, k2, k3, weights0, weights1, peaks_ref, top_ref, kseq, peak, mass
):
    sorted_blocks(meta_ref, (k0, k1, k2, k3), kseq, True)

    def span(a, rows, tiles):
        peak[...] = jnp.full_like(peak, NEG)
        mass[...] = jnp.zeros_like(mass)

        weights, peaks = (weights0, weights1)[a], peaks_ref.at[a]

        def stats(t, at, pick):
            k = kseq[pl.ds(at, TILE), :]
            for c in range(0, ROWS, 256):
                cols = pl.ds(c, 256)
                s = pick(nn(k, qt[:, pl.ds(a * ROWS + c, 256)]), NEG, c, 256)
                old = peak[:, cols]
                fresh = jnp.maximum(old, jnp.max(s, axis=0, keepdims=True))
                e = jnp.exp2(s * (SCALE * LOG2E) - fresh * (SCALE * LOG2E))
                mass[:, cols] = mass[:, cols] * jnp.exp2((old - fresh) * (SCALE * LOG2E)) + jnp.sum(
                    e, axis=0, keepdims=True
                )
                peak[:, cols] = fresh
                peaks[t, :, cols] = jnp.broadcast_to(fresh, (8, 256))
                weights[t, :, cols] = e

        tiles(stats)
        top_ref[pl.ds(a * 8, 4), :] = jnp.broadcast_to(peak[...], (4, ROWS))
        top_ref[pl.ds(a * 8 + 4, 4), :] = jnp.broadcast_to(mass[...], (4, ROWS))

    each_query_span(meta_ref, span)


def key_value_kernel(
    meta_ref, qs, gs, gt, delta_ref, top_ref, weights0, weights1, peaks_ref, v0, v1, v2, v3,
    dkv_ref, lse_ref, vseq, acc,
):
    sorted_blocks(meta_ref, (v0, v1, v2, v3), vseq, False)
    acc[...] = jnp.zeros_like(acc)

    def span(a, rows, tiles):
        high, mass = top_ref[pl.ds(a * 8, 1), :], top_ref[pl.ds(a * 8 + 4, 1), :]
        lse = high * (SCALE * LOG2E) + jnp.log2(mass)
        lse_ref[pl.ds(a * 8, 8), :] = jnp.broadcast_to(lse, (8, ROWS))
        inverse = 1.0 / mass
        delta = delta_ref[pl.ds(a * 8, 1), :]

        weights, peaks = (weights0, weights1)[a], peaks_ref.at[a]

        def step(t, at, pick):
            v = vseq[pl.ds(at, TILE), :]
            dk, dv = acc[pl.ds(at, TILE), :HD], acc[pl.ds(at, TILE), HD:]
            for c in range(0, ROWS, 256):
                cols, some = pl.ds(c, 256), pl.ds(a * ROWS + c, 256)
                w = jnp.exp2((peaks[t, :, cols][:1] - high[:, c : c + 256]) * (SCALE * LOG2E)) * inverse[:, c : c + 256]
                p = weights[t, :, cols] * w
                ds = p * (nn(v, gt[:, some]) - delta[:, c : c + 256])
                dv = dv + nn(p.astype(bf16), gs[some, :])
                dk = dk + nn(ds.astype(bf16), qs[some, :])
            acc[pl.ds(at, TILE), :HD] = dk
            acc[pl.ds(at, TILE), HD:] = dv

        tiles(step, masked=False)

    each_query_span(meta_ref, span)
    for slot in range(SPANS):
        at = slot_place(meta_ref, slot)
        row = pl.ds(slot * SPAN, SPAN)
        dkv_ref[row, :HD] = (acc[pl.ds(at, SPAN), :HD] * SCALE).astype(bf16)
        dkv_ref[row, HD:] = acc[pl.ds(at, SPAN), HD:].astype(bf16)


def query_kernel(
    meta_ref, qt, gt, delta_ref, lse_ref, k0, k1, k2, k3, v0, v1, v2, v3,
    dq_ref, sq_ref, kseq, vseq, acc,
):
    sorted_blocks(meta_ref, (k0, k1, k2, k3), kseq, True)
    sorted_blocks(meta_ref, (v0, v1, v2, v3), vseq, False)
    square = []

    def span(a, rows, tiles):
        lse, delta = lse_ref[pl.ds(a * 8, 1), :], delta_ref[pl.ds(a * 8, 1), :]
        acc[...] = jnp.zeros_like(acc)

        def step(t, at, pick):
            k = kseq[pl.ds(at, TILE), :]
            p = pick(jnp.exp2(nn(k, qt[:, rows]) * (SCALE * LOG2E) - lse), 0.0)
            ds = p * (nn(vseq[pl.ds(at, TILE), :], gt[:, rows]) - delta)
            acc[...] += tn(k, ds.astype(bf16))

        tiles(step)
        dq = (acc[...] * SCALE).T.astype(bf16)
        for h in range(GROUP):
            dq_ref[pl.ds(a * SPAN, SPAN), pl.ds(h * HD, HD)] = dq[h * SPAN : (h + 1) * SPAN]
        dq = dq.astype(f32)
        square.append(jnp.sum(jnp.sum(dq * dq, axis=0, keepdims=True), axis=1, keepdims=True))

    each_query_span(meta_ref, span)
    sq_ref[...] = jnp.broadcast_to(square[0] + square[1], sq_ref.shape)


def sum_kernel(parts_ref, other_ref):
    index = 1 - lax.axis_index("zh")
    total = parts_ref[0, index].astype(f32)
    for h in range(1, NY * NX):
        total = total + parts_ref[h, index].astype(f32)
    other_ref[...] = total.astype(bf16)


def finish_kernel(parts_ref, other_ref, sq_ref, dk_ref, dv_ref, local_ref):
    index = lax.axis_index("zh")
    total = parts_ref[0, index].astype(f32)
    for h in range(1, NY * NX):
        total = total + parts_ref[h, index].astype(f32)
    both = (total + other_ref[...].astype(f32)).astype(bf16)
    dk_ref[...] = both[:, :HD]
    dv_ref[...] = both[:, HD:]
    wide = both.astype(f32)
    local = jnp.sum(jnp.sum(wide * wide, axis=0, keepdims=True), axis=1, keepdims=True)
    local_ref[...] = jnp.broadcast_to((local + sq_ref[:1, :1])[None], local_ref.shape)


def call(kernel, outs, smem, scratch, flops, *args):
    vm = pl.BlockSpec(memory_space=pltpu.VMEM)
    sm = pl.BlockSpec(memory_space=pltpu.SMEM)
    return pl.pallas_call(
        kernel,
        out_shape=tuple(jax.ShapeDtypeStruct(s, t) for s, t in outs),
        in_specs=[sm] * smem + [vm] * (len(args) - smem),
        out_specs=(vm,) * len(outs),
        scratch_shapes=[pltpu.VMEM(s, t) for s, t in scratch],
        compiler_params=pltpu.CompilerParams(vmem_limit_bytes=VMEM),
        cost_estimate=pl.CostEstimate(flops=flops, bytes_accessed=4 << 20, transcendentals=0),
    )(*args)


def shift(a, axis, step):
    n = lax.axis_size(axis)
    return lax.ppermute(a, axis, [(i, (i + step) % n) for i in range(n)])


def shards(queries, keys, values, outputs, out_grad, doc_lengths, span_perm):
    tq = queries.shape[0]
    k = jnp.stack([keys, shift(keys, "zh", 1)])
    v = jnp.stack([values, shift(values, "zh", 1)])
    k = [k] + [shift(k, "x", s) for s in range(1, NX)]
    v = [v] + [shift(v, "y", s) for s in range(1, NY)]
    k, v = lax.optimization_barrier((k, v))
    k, v = jnp.stack(k), jnp.stack(v)
    k = [k] + [shift(k, "y", s) for s in range(1, NY)]
    v = [v] + [shift(v, "x", s) for s in range(1, NX)]
    k = [a.reshape(TOTAL // NY, HD) for a in k]
    v = [a.reshape(TOTAL // NX, HD) for a in v]

    meta = jnp.concatenate([span_perm, doc_lengths])
    heads, turned = ((2 * ROWS, HD), bf16), ((HD, 2 * ROWS), bf16)
    row, one, longer = ((16, ROWS), f32), ((1, ROWS), f32), ((TOTAL + TILE, HD), bf16)
    most = -(-(TOTAL // 2 + SPAN) // TILE)
    qs, gs, qt, gt, delta = call(
        prepare_kernel,
        [heads, heads, turned, turned, row],
        0, [], 1 << 30, queries, outputs, out_grad,
    )
    weights0, weights1, peaks, top = call(
        score_kernel,
        [((most, TILE, ROWS), f32), ((most, TILE, ROWS), f32), ((2, most, 8, ROWS), f32), row],
        1,
        [longer, one, one],
        8 << 30,
        meta, qt, *k,
    )
    parts, lse = call(
        key_value_kernel,
        [((TOTAL, 2 * HD), bf16), row],
        1,
        [longer, ((TOTAL + TILE, 2 * HD), f32)],
        16 << 30,
        meta, qs, gs, gt, delta, top, weights0, weights1, peaks, *v,
    )
    parts = parts.reshape(NY * NX, NZ, tq, 2 * HD)
    parts = lax.all_to_all(parts, ("y", "x"), 0, 0)
    query_grad, square = call(
        query_kernel,
        [(queries.shape, bf16), ((8, HD), f32)],
        1,
        [longer, longer, ((HD, ROWS), f32)],
        16 << 30,
        meta, qt, gt, delta, lse, *k, *v,
    )
    parts, query_grad, square = lax.optimization_barrier((parts, query_grad, square))
    half = ((tq, HD), bf16)
    (other,) = call(sum_kernel, [((tq, 2 * HD), bf16)], 0, [], 1 << 20, parts)
    every = ("y", "x", "zh", "tp")
    key_grad, value_grad, local = call(
        finish_kernel,
        [half, half, ((lax.axis_size(every), 1, HD), f32)],
        0, [], 1 << 20, parts, shift(other, "zh", 1), square,
    )
    grad_square = jnp.sum(lax.all_to_all(local, every, 0, 0)[:, 0, 0])
    return (query_grad, key_grad, value_grad, grad_square)


def solution(mesh):
    tp = mesh.devices.shape[1]
    split = Mesh(mesh.devices.reshape(NY, NX, NZ, tp), ("y", "x", "zh", "tp"))
    both = P(("y", "x", "zh"), "tp")
    return jax.shard_map(
        shards,
        mesh=split,
        in_specs=(both,) * 5 + (P(), P()),
        out_specs=(both, both, both, P()),
        check_vma=False,
    )
```

```python
import jax
import jax.numpy as jnp
from jax import lax
from jax.experimental import pallas as pl
from jax.experimental.pallas import tpu as pltpu
from jax.sharding import Mesh
from jax.sharding import PartitionSpec as P

HD = 128
GROUP = 16
SPAN = 64
SPANS = 64
NY, NX, NZ = 4, 4, 2
ROWS = SPAN * GROUP
TILE = 512
TOTAL = SPAN * SPANS
SCALE = HD ** (-0.5)
LOG2E = 1.4426950408889634
NEG = -1e30
PARTS = 8

f32, bf16, i32 = jnp.float32, jnp.bfloat16, jnp.int32


def nt(a, b):
    return lax.dot_general(a, b, (((1,), (1,)), ((), ())), preferred_element_type=f32)


def nn(a, b):
    return lax.dot_general(a, b, (((1,), (0,)), ((), ())), preferred_element_type=f32)


def tn(a, b):
    return lax.dot_general(a, b, (((0,), (0,)), ((), ())), preferred_element_type=f32)


def position():
    y, x, z = lax.axis_index("y"), lax.axis_index("x"), lax.axis_index("zh")
    return y, x, z, (y * NX + x) * NZ + z


def slot_place(meta_ref, slot):
    return pl.multiple_of(meta_ref[slot] * SPAN, SPAN)


def each_query_span(meta_ref, body):
    me = position()[3]
    ends, total = [], 0
    for d in range(meta_ref.shape[0] - SPANS):
        total = total + meta_ref[SPANS + d]
        ends.append(total)
    lane = lax.broadcasted_iota(i32, (1, ROWS), 1)
    for a in range(2):
        span = meta_ref[me * 2 + a]
        place = span * SPAN + (lane & (SPAN - 1))
        begin = jnp.zeros_like(place)
        first, last = 0, 0
        for end in ends:
            begin = jnp.maximum(begin, jnp.where(end <= place, end, 0))
            first = jnp.maximum(first, jnp.where(end <= span * SPAN, end, 0))
            last = jnp.maximum(last, jnp.where(end <= span * SPAN + SPAN - 1, end, 0))
        start = (first // SPAN) * SPAN
        count = (span * SPAN + SPAN - start + TILE - 1) // TILE

        def visible(k0, c, n, place=place, begin=begin):
            kp = k0 + lax.broadcasted_iota(i32, (TILE, 1), 0)
            return (kp <= place[:, c : c + n]) & (kp >= begin[:, c : c + n])

        def tiles(step, masked=True, start=start, count=count, span=span, last=last):
            def one(t, carry):
                k0 = pl.multiple_of(start + t * TILE, SPAN)
                whole = (k0 >= last) & (k0 + TILE <= span * SPAN + 1)
                if not masked:
                    step(t, k0, None)
                    return carry

                @pl.when(whole)
                def _():
                    step(t, k0, lambda a, b, c=0, n=ROWS: a)

                @pl.when(jnp.logical_not(whole))
                def _():
                    step(t, k0, lambda a, b, c=0, n=ROWS: jnp.where(visible(k0, c, n), a, b))

                return carry

            lax.fori_loop(0, count, one, 0)

        body(a, pl.ds(a * ROWS, ROWS), tiles)


def sorted_blocks(meta_ref, pieces, seq, keys):
    y, x, z, _ = position()
    for sy in range(NY):
        for sx in range(NX):
            for zz in range(NZ * 2):
                home = ((y + NY - sy) % NY) * NX + (x + NX - sx) % NX
                at = slot_place(meta_ref, (home * NZ + (z + zz // 2) % NZ) * 2 + zz % 2)
                last, inner = (sy, sx) if keys else (sx, sy)
                row = pl.ds((inner * 2 * NZ + zz) * SPAN, SPAN)
                seq[pl.ds(at, SPAN), :] = pieces[last][row, :]
    seq[pl.ds(TOTAL, TILE), :] = jnp.zeros((TILE, HD), bf16)


def prepare_kernel(q_hbm, o_hbm, g_hbm, qs, gs, qt, gt, delta, q_ref, o_ref, g_ref, sems):
    copies = [
        pltpu.make_async_copy(s, d, sems.at[i])
        for i, (s, d) in enumerate(((q_hbm, q_ref), (o_hbm, o_ref), (g_hbm, g_ref)))
    ]
    for c in copies:
        c.start()
    for c in copies:
        c.wait()
    for a in range(2):
        prods = []
        for h in range(GROUP):
            dst = pl.ds(a * ROWS + h * SPAN, SPAN)
            src = (pl.ds(a * SPAN, SPAN), pl.ds(h * HD, HD))
            qs[dst, :] = q_ref[src]
            gs[dst, :] = g_ref[src]
            prods.append(g_ref[src].astype(f32) * o_ref[src].astype(f32))
        rows = pl.ds(a * ROWS, ROWS)
        qt[:, rows] = qs[rows, :].T
        gt[:, rows] = gs[rows, :].T
        prod = jnp.concatenate(prods, axis=0)
        high = prod.astype(bf16)
        low = (prod - high.astype(f32)).astype(bf16)
        ones = jnp.ones((16, HD), bf16)
        delta[pl.ds(a * 8, 8), :] = (nt(ones, high) + nt(ones, low))[:8]


def score_kernel(
    meta_ref, qt, k0, k1, k2, k3, weights0, weights1, peaks_ref, top_ref, kseq, peak, mass
):
    sorted_blocks(meta_ref, (k0, k1, k2, k3), kseq, True)

    def span(a, rows, tiles):
        peak[...] = jnp.full_like(peak, NEG)
        mass[...] = jnp.zeros_like(mass)

        weights, peaks = (weights0, weights1)[a], peaks_ref.at[a]

        def stats(t, at, pick):
            k = kseq[pl.ds(at, TILE), :]
            for c in range(0, ROWS, 256):
                cols = pl.ds(c, 256)
                s = pick(nn(k, qt[:, pl.ds(a * ROWS + c, 256)]), NEG, c, 256)
                old = peak[:, cols]
                fresh = jnp.maximum(old, jnp.max(s, axis=0, keepdims=True))
                e = jnp.exp2(s * (SCALE * LOG2E) - fresh * (SCALE * LOG2E))
                mass[:, cols] = mass[:, cols] * jnp.exp2((old - fresh) * (SCALE * LOG2E)) + jnp.sum(
                    e, axis=0, keepdims=True
                )
                peak[:, cols] = fresh
                peaks[t, :, cols] = jnp.broadcast_to(fresh, (8, 256))
                weights[t, :, cols] = e

        tiles(stats)
        top_ref[pl.ds(a * 8, 4), :] = jnp.broadcast_to(peak[...], (4, ROWS))
        top_ref[pl.ds(a * 8 + 4, 4), :] = jnp.broadcast_to(mass[...], (4, ROWS))

    each_query_span(meta_ref, span)


def key_value_kernel(
    meta_ref, qs, gs, gt, delta_ref, top_ref, weights0, weights1, peaks_ref, v0, v1, v2, v3,
    dkv_hbm, lse_ref, vseq, acc, out, sems,
):
    sorted_blocks(meta_ref, (v0, v1, v2, v3), vseq, False)
    acc[...] = jnp.zeros_like(acc)

    def span(a, rows, tiles):
        high, mass = top_ref[pl.ds(a * 8, 1), :], top_ref[pl.ds(a * 8 + 4, 1), :]
        lse = high * (SCALE * LOG2E) + jnp.log2(mass)
        lse_ref[pl.ds(a * 8, 8), :] = jnp.broadcast_to(lse, (8, ROWS))
        inverse = 1.0 / mass
        delta = delta_ref[pl.ds(a * 8, 1), :]

        weights, peaks = (weights0, weights1)[a], peaks_ref.at[a]

        def step(t, at, pick):
            v = vseq[pl.ds(at, TILE), :]
            dk, dv = acc[pl.ds(at, TILE), :HD], acc[pl.ds(at, TILE), HD:]
            for c in range(0, ROWS, 256):
                cols, some = pl.ds(c, 256), pl.ds(a * ROWS + c, 256)
                w = jnp.exp2((peaks[t, :, cols][:1] - high[:, c : c + 256]) * (SCALE * LOG2E)) * inverse[:, c : c + 256]
                p = weights[t, :, cols] * w
                ds = p * (nn(v, gt[:, some]) - delta[:, c : c + 256])
                dv = dv + nn(p.astype(bf16), gs[some, :])
                dk = dk + nn(ds.astype(bf16), qs[some, :])
            acc[pl.ds(at, TILE), :HD] = dk
            acc[pl.ds(at, TILE), HD:] = dv

        tiles(step, masked=False)

    each_query_span(meta_ref, span)
    copies = []
    for part in range(PARTS):
        for slot in range(part * SPANS // PARTS, (part + 1) * SPANS // PARTS):
            at = slot_place(meta_ref, slot)
            row = pl.ds(slot * SPAN, SPAN)
            out[row, :HD] = (acc[pl.ds(at, SPAN), :HD] * SCALE).astype(bf16)
            out[row, HD:] = acc[pl.ds(at, SPAN), HD:].astype(bf16)
        rows = pl.ds(part * TOTAL // PARTS, TOTAL // PARTS)
        copies.append(pltpu.make_async_copy(out.at[rows], dkv_hbm.at[rows], sems.at[part]))
        copies[-1].start()
    for c in copies:
        c.wait()


def query_kernel(
    meta_ref, qt, gt, delta_ref, lse_ref, k0, k1, k2, k3, v0, v1, v2, v3,
    dq_ref, sq_ref, kseq, vseq, acc,
):
    sorted_blocks(meta_ref, (k0, k1, k2, k3), kseq, True)
    sorted_blocks(meta_ref, (v0, v1, v2, v3), vseq, False)
    square = []

    def span(a, rows, tiles):
        lse, delta = lse_ref[pl.ds(a * 8, 1), :], delta_ref[pl.ds(a * 8, 1), :]
        acc[...] = jnp.zeros_like(acc)

        def step(t, at, pick):
            k = kseq[pl.ds(at, TILE), :]
            p = pick(jnp.exp2(nn(k, qt[:, rows]) * (SCALE * LOG2E) - lse), 0.0)
            ds = p * (nn(vseq[pl.ds(at, TILE), :], gt[:, rows]) - delta)
            acc[...] += tn(k, ds.astype(bf16))

        tiles(step)
        dq = (acc[...] * SCALE).T.astype(bf16)
        for h in range(GROUP):
            dq_ref[pl.ds(a * SPAN, SPAN), pl.ds(h * HD, HD)] = dq[h * SPAN : (h + 1) * SPAN]
        dq = dq.astype(f32)
        square.append(jnp.sum(jnp.sum(dq * dq, axis=0, keepdims=True), axis=1, keepdims=True))

    each_query_span(meta_ref, span)
    sq_ref[...] = jnp.broadcast_to(square[0] + square[1], sq_ref.shape)


def sum_kernel(parts_ref, other_ref):
    index = 1 - lax.axis_index("zh")
    total = parts_ref[0, index].astype(f32)
    for h in range(1, NY * NX):
        total = total + parts_ref[h, index].astype(f32)
    other_ref[...] = total.astype(bf16)


def finish_kernel(parts_ref, other_ref, sq_ref, dk_ref, dv_ref, local_ref):
    index = lax.axis_index("zh")
    total = parts_ref[0, index].astype(f32)
    for h in range(1, NY * NX):
        total = total + parts_ref[h, index].astype(f32)
    both = (total + other_ref[...].astype(f32)).astype(bf16)
    dk_ref[...] = both[:, :HD]
    dv_ref[...] = both[:, HD:]
    wide = both.astype(f32)
    local = jnp.sum(jnp.sum(wide * wide, axis=0, keepdims=True), axis=1, keepdims=True)
    local_ref[...] = jnp.broadcast_to((local + sq_ref[:1, :1])[None], local_ref.shape)


def call(kernel, outs, specs, scratch, flops, limit, *args):
    kind = {
        "S": pl.BlockSpec(memory_space=pltpu.SMEM),
        "H": pl.BlockSpec(memory_space=pl.ANY),
        "V": pl.BlockSpec(memory_space=pltpu.VMEM),
    }
    given, made = specs.split()
    args = [
        pltpu.with_memory_space_constraint(a, pltpu.HBM) if c == "H" else a
        for a, c in zip(args, given, strict=True)
    ]
    return pl.pallas_call(
        kernel,
        out_shape=tuple(
            pltpu.HBM(s, t) if c == "H" else jax.ShapeDtypeStruct(s, t)
            for (s, t), c in zip(outs, made, strict=True)
        ),
        in_specs=[kind[c] for c in given],
        out_specs=tuple(kind[c] for c in made),
        scratch_shapes=[
            pltpu.SemaphoreType.DMA(s) if t is None else pltpu.VMEM(s, t) for s, t in scratch
        ],
        compiler_params=pltpu.CompilerParams(vmem_limit_bytes=limit << 20),
        cost_estimate=pl.CostEstimate(flops=flops, bytes_accessed=4 << 20, transcendentals=0),
    )(*args)


def shift(a, axis, step):
    n = lax.axis_size(axis)
    return lax.ppermute(a, axis, [(i, (i + step) % n) for i in range(n)])


def shards(queries, keys, values, outputs, out_grad, doc_lengths, span_perm):
    tq = queries.shape[0]
    meta = jnp.concatenate([span_perm, doc_lengths])
    kv = jnp.stack([keys, values])
    kv = jnp.stack([kv, shift(kv, "zh", 1)], axis=1)
    k, v = kv[0], kv[1]
    k = [k] + [shift(k, "x", s) for s in range(1, NX)]
    v = [v] + [shift(v, "y", s) for s in range(1, NY)]
    mine = (queries.shape, bf16)
    heads, turned = ((2 * ROWS, HD), bf16), ((HD, 2 * ROWS), bf16)
    row, one, longer = ((16, ROWS), f32), ((1, ROWS), f32), ((TOTAL + TILE, HD), bf16)
    most = -(-(TOTAL // 2 + SPAN) // TILE)
    ready = call(
        prepare_kernel,
        [heads, heads, turned, turned, row],
        "HHH VVVVV",
        [mine, mine, mine, ((3,), None)],
        1 << 30, 16, queries, outputs, out_grad,
    )
    k, v, meta = lax.optimization_barrier((k, v, meta))
    qs, gs, qt, gt, delta = ready
    k, v = jnp.stack(k), jnp.stack(v)
    k = [k] + [shift(k, "y", s) for s in range(1, NY)]
    v = [v] + [shift(v, "x", s) for s in range(1, NX)]
    k = [a.reshape(TOTAL // NY, HD) for a in k]
    v = [a.reshape(TOTAL // NX, HD) for a in v]

    weights0, weights1, peaks, top = call(
        score_kernel,
        [((most, TILE, ROWS), f32), ((most, TILE, ROWS), f32), ((2, most, 8, ROWS), f32), row],
        "SVVVVV VVVV",
        [longer, one, one],
        8 << 30, 16, meta, qt, *k,
    )
    parts, lse = call(
        key_value_kernel,
        [((TOTAL, 2 * HD), bf16), row],
        "SVVVVVVVVVVVV HV",
        [longer, ((TOTAL + TILE, 2 * HD), f32), ((TOTAL, 2 * HD), bf16), ((PARTS,), None)],
        16 << 30, 16, meta, qs, gs, gt, delta, top, weights0, weights1, peaks, *v,
    )
    parts = parts.reshape(NY * NX, NZ, tq, 2 * HD)
    parts = lax.all_to_all(parts, ("y", "x"), 0, 0)
    query_grad, square = call(
        query_kernel,
        [mine, ((8, HD), f32)],
        "SVVVVVVVVVVVV VV",
        [longer, longer, ((HD, ROWS), f32)],
        16 << 30, 32, meta, qt, gt, delta, lse, *k, *v,
    )
    parts, query_grad, square = lax.optimization_barrier((parts, query_grad, square))
    half = ((tq, HD), bf16)
    (other,) = call(sum_kernel, [((tq, 2 * HD), bf16)], "V V", [], 1 << 20, 16, parts)
    every = ("y", "x", "zh", "tp")
    key_grad, value_grad, local = call(
        finish_kernel,
        [half, half, ((lax.axis_size(every), 1, HD), f32)],
        "VVV VVV",
        [], 1 << 20, 16, parts, shift(other, "zh", 1), square,
    )
    grad_square = jnp.sum(lax.all_to_all(local, every, 0, 0)[:, 0, 0])
    return (query_grad, key_grad, value_grad, grad_square)


def solution(mesh):
    tp = mesh.devices.shape[1]
    split = Mesh(mesh.devices.reshape(NY, NX, NZ, tp), ("y", "x", "zh", "tp"))
    both = P(("y", "x", "zh"), "tp")
    return jax.shard_map(
        shards,
        mesh=split,
        in_specs=(both,) * 5 + (P(), P()),
        out_specs=(both, both, both, P()),
        check_vma=False,
    )
```

```python
import jax
import jax.numpy as jnp
from jax import lax
from jax.experimental import pallas as pl
from jax.experimental.pallas import tpu as pltpu
from jax.sharding import Mesh
from jax.sharding import PartitionSpec as P

HD = 128
GROUP = 16
SPAN = 64
SPANS = 64
NY, NX, NZ = 4, 4, 2
ROWS = SPAN * GROUP
TILE = 704
TOTAL = SPAN * SPANS
SCALE = HD ** (-0.5)
LOG2E = 1.4426950408889634
NEG = -1e30
PARTS = 8

f32, bf16, i32 = jnp.float32, jnp.bfloat16, jnp.int32


def nt(a, b):
    return lax.dot_general(a, b, (((1,), (1,)), ((), ())), preferred_element_type=f32)


def nn(a, b):
    return lax.dot_general(a, b, (((1,), (0,)), ((), ())), preferred_element_type=f32)


def tn(a, b):
    return lax.dot_general(a, b, (((0,), (0,)), ((), ())), preferred_element_type=f32)


def position():
    y, x, z = lax.axis_index("y"), lax.axis_index("x"), lax.axis_index("zh")
    return y, x, z, (y * NX + x) * NZ + z


def slot_place(meta_ref, slot):
    return pl.multiple_of(meta_ref[slot] * SPAN, SPAN)


def each_query_span(meta_ref, body):
    me = position()[3]
    ends, total = [], 0
    for d in range(meta_ref.shape[0] - SPANS):
        total = total + meta_ref[SPANS + d]
        ends.append(total)
    lane = lax.broadcasted_iota(i32, (1, ROWS), 1)
    for a in range(2):
        span = meta_ref[me * 2 + a]
        place = span * SPAN + (lane & (SPAN - 1))
        begin = jnp.zeros_like(place)
        first, last = 0, 0
        for end in ends:
            begin = jnp.maximum(begin, jnp.where(end <= place, end, 0))
            first = jnp.maximum(first, jnp.where(end <= span * SPAN, end, 0))
            last = jnp.maximum(last, jnp.where(end <= span * SPAN + SPAN - 1, end, 0))
        start = (first // SPAN) * SPAN
        count = (span * SPAN + SPAN - start + TILE - 1) // TILE

        def visible(k0, c, n, place=place, begin=begin):
            kp = k0 + lax.broadcasted_iota(i32, (TILE, 1), 0)
            return (kp <= place[:, c : c + n]) & (kp >= begin[:, c : c + n])

        def tiles(step, masked=True, start=start, count=count, span=span, last=last):
            def one(t, carry):
                k0 = pl.multiple_of(start + t * TILE, SPAN)
                whole = (k0 >= last) & (k0 + TILE <= span * SPAN + 1)
                if not masked:
                    step(t, k0, None)
                    return carry

                @pl.when(whole)
                def _():
                    step(t, k0, lambda a, b, c=0, n=ROWS: a)

                @pl.when(jnp.logical_not(whole))
                def _():
                    step(t, k0, lambda a, b, c=0, n=ROWS: jnp.where(visible(k0, c, n), a, b))

                return carry

            lax.fori_loop(0, count, one, 0)

        body(a, pl.ds(a * ROWS, ROWS), tiles)


def sorted_blocks(meta_ref, pieces, seq, keys):
    y, x, z, _ = position()
    for sy in range(NY):
        for sx in range(NX):
            for zz in range(NZ * 2):
                home = ((y + NY - sy) % NY) * NX + (x + NX - sx) % NX
                at = slot_place(meta_ref, (home * NZ + (z + zz // 2) % NZ) * 2 + zz % 2)
                last, inner = (sx, sy) if keys else (sy, sx)
                row = pl.ds((inner * 2 * NZ + zz) * SPAN, SPAN)
                seq[pl.ds(at, SPAN), :] = pieces[last][row, :]
    seq[pl.ds(TOTAL, TILE), :] = jnp.zeros((TILE, HD), bf16)


def prepare_kernel(q_hbm, o_hbm, g_hbm, qs, gs, qt, gt, delta, q_ref, o_ref, g_ref, sems):
    copies = [
        pltpu.make_async_copy(s, d, sems.at[i])
        for i, (s, d) in enumerate(((q_hbm, q_ref), (o_hbm, o_ref), (g_hbm, g_ref)))
    ]
    for c in copies:
        c.start()
    for c in copies:
        c.wait()
    for a in range(2):
        prods = []
        for h in range(GROUP):
            dst = pl.ds(a * ROWS + h * SPAN, SPAN)
            src = (pl.ds(a * SPAN, SPAN), pl.ds(h * HD, HD))
            qs[dst, :] = q_ref[src]
            gs[dst, :] = g_ref[src]
            prods.append(g_ref[src].astype(f32) * o_ref[src].astype(f32))
        rows = pl.ds(a * ROWS, ROWS)
        qt[:, rows] = qs[rows, :].T
        gt[:, rows] = gs[rows, :].T
        prod = jnp.concatenate(prods, axis=0)
        high = prod.astype(bf16)
        low = (prod - high.astype(f32)).astype(bf16)
        ones = jnp.ones((16, HD), bf16)
        delta[pl.ds(a * 8, 8), :] = (nt(ones, high) + nt(ones, low))[:8]


def score_kernel(
    meta_ref, qt, k0, k1, k2, k3, weights0, weights1, peaks_ref, top_ref, kseq, peak, mass
):
    sorted_blocks(meta_ref, (k0, k1, k2, k3), kseq, True)

    def span(a, rows, tiles):
        peak[...] = jnp.full_like(peak, NEG)
        mass[...] = jnp.zeros_like(mass)

        weights, peaks = (weights0, weights1)[a], peaks_ref.at[a]

        def stats(t, at, pick):
            k = kseq[pl.ds(at, TILE), :]
            for c in range(0, ROWS, 256):
                cols = pl.ds(c, 256)
                s = pick(nn(k, qt[:, pl.ds(a * ROWS + c, 256)]), NEG, c, 256)
                old = peak[:, cols]
                fresh = jnp.maximum(old, jnp.max(s, axis=0, keepdims=True))
                e = jnp.exp2(s * (SCALE * LOG2E) - fresh * (SCALE * LOG2E))
                mass[:, cols] = mass[:, cols] * jnp.exp2((old - fresh) * (SCALE * LOG2E)) + jnp.sum(
                    e, axis=0, keepdims=True
                )
                peak[:, cols] = fresh
                peaks[t, :, cols] = jnp.broadcast_to(fresh, (8, 256))
                weights[t, :, cols] = e

        tiles(stats)
        top_ref[pl.ds(a * 8, 4), :] = jnp.broadcast_to(peak[...], (4, ROWS))
        top_ref[pl.ds(a * 8 + 4, 4), :] = jnp.broadcast_to(mass[...], (4, ROWS))

    each_query_span(meta_ref, span)


def key_value_kernel(
    meta_ref, qs, gs, gt, delta_ref, top_ref, weights0, weights1, peaks_ref, v0, v1, v2, v3,
    dkv_hbm, lse_ref, vseq, acc, out, sems,
):
    sorted_blocks(meta_ref, (v0, v1, v2, v3), vseq, False)
    acc[...] = jnp.zeros_like(acc)

    def span(a, rows, tiles):
        high, mass = top_ref[pl.ds(a * 8, 1), :], top_ref[pl.ds(a * 8 + 4, 1), :]
        lse = high * (SCALE * LOG2E) + jnp.log2(mass)
        lse_ref[pl.ds(a * 8, 8), :] = jnp.broadcast_to(lse, (8, ROWS))
        inverse = 1.0 / mass
        delta = delta_ref[pl.ds(a * 8, 1), :]

        weights, peaks = (weights0, weights1)[a], peaks_ref.at[a]

        def step(t, at, pick):
            v = vseq[pl.ds(at, TILE), :]
            dk, dv = acc[pl.ds(at, TILE), :HD], acc[pl.ds(at, TILE), HD:]
            for c in range(0, ROWS, 256):
                cols, some = pl.ds(c, 256), pl.ds(a * ROWS + c, 256)
                w = jnp.exp2((peaks[t, :, cols][:1] - high[:, c : c + 256]) * (SCALE * LOG2E)) * inverse[:, c : c + 256]
                p = weights[t, :, cols] * w
                ds = p * (nn(v, gt[:, some]) - delta[:, c : c + 256])
                dv = dv + nn(p.astype(bf16), gs[some, :])
                dk = dk + nn(ds.astype(bf16), qs[some, :])
            acc[pl.ds(at, TILE), :HD] = dk
            acc[pl.ds(at, TILE), HD:] = dv

        tiles(step, masked=False)

    each_query_span(meta_ref, span)
    copies = []
    for part in range(PARTS):
        for slot in range(part * SPANS // PARTS, (part + 1) * SPANS // PARTS):
            at = slot_place(meta_ref, slot)
            row = pl.ds(slot * SPAN, SPAN)
            out[row, :HD] = (acc[pl.ds(at, SPAN), :HD] * SCALE).astype(bf16)
            out[row, HD:] = acc[pl.ds(at, SPAN), HD:].astype(bf16)
        rows = pl.ds(part * TOTAL // PARTS, TOTAL // PARTS)
        copies.append(pltpu.make_async_copy(out.at[rows], dkv_hbm.at[rows], sems.at[part]))
        copies[-1].start()
    for c in copies:
        c.wait()


def query_kernel(
    meta_ref, qt, gt, delta_ref, lse_ref, k0, k1, k2, k3, v0, v1, v2, v3,
    dq_ref, sq_ref, kseq, vseq, acc,
):
    sorted_blocks(meta_ref, (k0, k1, k2, k3), kseq, True)
    sorted_blocks(meta_ref, (v0, v1, v2, v3), vseq, False)
    square = []

    def span(a, rows, tiles):
        lse, delta = lse_ref[pl.ds(a * 8, 1), :], delta_ref[pl.ds(a * 8, 1), :]
        acc[...] = jnp.zeros_like(acc)

        def step(t, at, pick):
            k = kseq[pl.ds(at, TILE), :]
            p = pick(jnp.exp2(nn(k, qt[:, rows]) * (SCALE * LOG2E) - lse), 0.0)
            ds = p * (nn(vseq[pl.ds(at, TILE), :], gt[:, rows]) - delta)
            acc[...] += tn(k, ds.astype(bf16))

        tiles(step)
        dq = (acc[...] * SCALE).T.astype(bf16)
        for h in range(GROUP):
            dq_ref[pl.ds(a * SPAN, SPAN), pl.ds(h * HD, HD)] = dq[h * SPAN : (h + 1) * SPAN]
        dq = dq.astype(f32)
        square.append(jnp.sum(jnp.sum(dq * dq, axis=0, keepdims=True), axis=1, keepdims=True))

    each_query_span(meta_ref, span)
    sq_ref[...] = jnp.broadcast_to(square[0] + square[1], sq_ref.shape)


def sum_kernel(parts_ref, other_ref):
    index = 1 - lax.axis_index("zh")
    total = parts_ref[0, index].astype(f32)
    for h in range(1, NY * NX):
        total = total + parts_ref[h, index].astype(f32)
    other_ref[...] = total.astype(bf16)


def finish_kernel(parts_ref, other_ref, sq_ref, dk_ref, dv_ref, local_ref):
    index = lax.axis_index("zh")
    total = parts_ref[0, index].astype(f32)
    for h in range(1, NY * NX):
        total = total + parts_ref[h, index].astype(f32)
    both = (total + other_ref[...].astype(f32)).astype(bf16)
    dk_ref[...] = both[:, :HD]
    dv_ref[...] = both[:, HD:]
    wide = both.astype(f32)
    local = jnp.sum(jnp.sum(wide * wide, axis=0, keepdims=True), axis=1, keepdims=True)
    local_ref[...] = jnp.broadcast_to((local + sq_ref[:1, :1])[None], local_ref.shape)


def call(kernel, outs, specs, scratch, flops, limit, *args):
    kind = {
        "S": pl.BlockSpec(memory_space=pltpu.SMEM),
        "H": pl.BlockSpec(memory_space=pl.ANY),
        "V": pl.BlockSpec(memory_space=pltpu.VMEM),
    }
    given, made = specs.split()
    args = [
        pltpu.with_memory_space_constraint(a, pltpu.HBM) if c == "H" else a
        for a, c in zip(args, given, strict=True)
    ]
    return pl.pallas_call(
        kernel,
        out_shape=tuple(
            pltpu.HBM(s, t) if c == "H" else jax.ShapeDtypeStruct(s, t)
            for (s, t), c in zip(outs, made, strict=True)
        ),
        in_specs=[kind[c] for c in given],
        out_specs=tuple(kind[c] for c in made),
        scratch_shapes=[
            pltpu.SemaphoreType.DMA(s) if t is None else pltpu.VMEM(s, t) for s, t in scratch
        ],
        compiler_params=pltpu.CompilerParams(vmem_limit_bytes=limit << 20),
        cost_estimate=pl.CostEstimate(flops=flops, bytes_accessed=4 << 20, transcendentals=0),
    )(*args)


def shift(a, axis, step):
    n = lax.axis_size(axis)
    return lax.ppermute(a, axis, [(i, (i + step) % n) for i in range(n)])


def shards(queries, keys, values, outputs, out_grad, doc_lengths, span_perm):
    tq = queries.shape[0]
    meta = jnp.concatenate([span_perm, doc_lengths])
    kv = jnp.stack([keys, values])
    kv = jnp.stack([kv, shift(kv, "zh", 1)], axis=1)
    k, v = kv[0], kv[1]
    k = [k] + [shift(k, "y", s) for s in range(1, NY)]
    v = [v] + [shift(v, "x", s) for s in range(1, NX)]
    mine = (queries.shape, bf16)
    heads, turned = ((2 * ROWS, HD), bf16), ((HD, 2 * ROWS), bf16)
    row, one, longer = ((16, ROWS), f32), ((1, ROWS), f32), ((TOTAL + TILE, HD), bf16)
    most = -(-(TOTAL // 2 + SPAN) // TILE)
    ready = call(
        prepare_kernel,
        [heads, heads, turned, turned, row],
        "HHH VVVVV",
        [mine, mine, mine, ((3,), None)],
        1 << 30, 16, queries, outputs, out_grad,
    )
    k, v, meta = lax.optimization_barrier((k, v, meta))
    qs, gs, qt, gt, delta = ready
    k, v = jnp.stack(k), jnp.stack(v)
    k = [k] + [shift(k, "x", s) for s in range(1, NX)]
    v = [v] + [shift(v, "y", s) for s in range(1, NY)]
    k = [a.reshape(TOTAL // NY, HD) for a in k]
    v = [a.reshape(TOTAL // NX, HD) for a in v]

    weights0, weights1, peaks, top = call(
        score_kernel,
        [((most, TILE, ROWS), f32), ((most, TILE, ROWS), f32), ((2, most, 8, ROWS), f32), row],
        "SVVVVV VVVV",
        [longer, one, one],
        8 << 30, 16, meta, qt, *k,
    )
    parts, lse = call(
        key_value_kernel,
        [((TOTAL, 2 * HD), bf16), row],
        "SVVVVVVVVVVVV HV",
        [longer, ((TOTAL + TILE, 2 * HD), f32), ((TOTAL, 2 * HD), bf16), ((PARTS,), None)],
        16 << 30, 16, meta, qs, gs, gt, delta, top, weights0, weights1, peaks, *v,
    )
    parts = parts.reshape(NY * NX, NZ, tq, 2 * HD)
    parts = lax.all_to_all(parts, ("y", "x"), 0, 0)
    query_grad, square = call(
        query_kernel,
        [mine, ((8, HD), f32)],
        "SVVVVVVVVVVVV VV",
        [longer, longer, ((HD, ROWS), f32)],
        16 << 30, 32, meta, qt, gt, delta, lse, *k, *v,
    )
    parts, query_grad, square = lax.optimization_barrier((parts, query_grad, square))
    half = ((tq, HD), bf16)
    (other,) = call(sum_kernel, [((tq, 2 * HD), bf16)], "V V", [], 1 << 20, 16, parts)
    every = ("y", "x", "zh", "tp")
    key_grad, value_grad, local = call(
        finish_kernel,
        [half, half, ((lax.axis_size(every), 1, HD), f32)],
        "VVV VVV",
        [], 1 << 20, 16, parts, shift(other, "zh", 1), square,
    )
    grad_square = jnp.sum(lax.all_to_all(local, every, 0, 0)[:, 0, 0])
    return (query_grad, key_grad, value_grad, grad_square)


def solution(mesh):
    tp = mesh.devices.shape[1]
    split = Mesh(mesh.devices.reshape(NY, NX, NZ, tp), ("y", "x", "zh", "tp"))
    both = P(("y", "x", "zh"), "tp")
    return jax.shard_map(
        shards,
        mesh=split,
        in_specs=(both,) * 5 + (P(), P()),
        out_specs=(both, both, both, P()),
        check_vma=False,
    )
```

```python
import jax
import jax.numpy as jnp
from jax import lax
from jax.experimental import pallas as pl
from jax.experimental.pallas import tpu as pltpu
from jax.sharding import Mesh
from jax.sharding import PartitionSpec as P

HD = 128
GROUP = 16
SPAN = 64
SPANS = 64
NY, NX, NZ = 4, 4, 2
ROWS = SPAN * GROUP
TILE = 704
TOTAL = SPAN * SPANS
SCALE = HD ** (-0.5)
LOG2E = 1.4426950408889634
NEG = -1e30
PARTS = 8

f32, bf16, i32 = jnp.float32, jnp.bfloat16, jnp.int32


def nt(a, b):
    return lax.dot_general(a, b, (((1,), (1,)), ((), ())), preferred_element_type=f32)


def nn(a, b):
    return lax.dot_general(a, b, (((1,), (0,)), ((), ())), preferred_element_type=f32)


def tn(a, b):
    return lax.dot_general(a, b, (((0,), (0,)), ((), ())), preferred_element_type=f32)


def position():
    y, x, z = lax.axis_index("y"), lax.axis_index("x"), lax.axis_index("zh")
    return y, x, z, (y * NX + x) * NZ + z


def slot_place(meta_ref, slot):
    return pl.multiple_of(meta_ref[slot] * SPAN, SPAN)


def each_query_span(meta_ref, body):
    me = position()[3]
    ends, total = [], 0
    for d in range(meta_ref.shape[0] - SPANS):
        total = total + meta_ref[SPANS + d]
        ends.append(total)
    lane = lax.broadcasted_iota(i32, (1, ROWS), 1)
    for a in range(2):
        span = meta_ref[me * 2 + a]
        place = span * SPAN + (lane & (SPAN - 1))
        begin = jnp.zeros_like(place)
        first, last = 0, 0
        for end in ends:
            begin = jnp.maximum(begin, jnp.where(end <= place, end, 0))
            first = jnp.maximum(first, jnp.where(end <= span * SPAN, end, 0))
            last = jnp.maximum(last, jnp.where(end <= span * SPAN + SPAN - 1, end, 0))
        start = (first // SPAN) * SPAN
        count = (span * SPAN + SPAN - start + TILE - 1) // TILE

        def visible(k0, c, n, place=place, begin=begin):
            kp = k0 + lax.broadcasted_iota(i32, (TILE, 1), 0)
            return (kp <= place[:, c : c + n]) & (kp >= begin[:, c : c + n])

        def tiles(step, masked=True, start=start, count=count, span=span, last=last):
            def one(t, carry):
                k0 = pl.multiple_of(start + t * TILE, SPAN)
                whole = (k0 >= last) & (k0 + TILE <= span * SPAN + 1)
                if not masked:
                    step(t, k0, None)
                    return carry

                @pl.when(whole)
                def _():
                    step(t, k0, lambda a, b, c=0, n=ROWS: a)

                @pl.when(jnp.logical_not(whole))
                def _():
                    step(t, k0, lambda a, b, c=0, n=ROWS: jnp.where(visible(k0, c, n), a, b))

                return carry

            lax.fori_loop(0, count, one, 0)

        body(a, pl.ds(a * ROWS, ROWS), tiles)


def sorted_blocks(meta_ref, pieces, seq, keys):
    y, x, z, _ = position()
    for sy in range(NY):
        for sx in range(NX):
            for zz in range(NZ * 2):
                home = ((y + NY - sy) % NY) * NX + (x + NX - sx) % NX
                at = slot_place(meta_ref, (home * NZ + (z + zz // 2) % NZ) * 2 + zz % 2)
                last, inner = (sx, sy) if keys else (sy, sx)
                row = pl.ds((inner * 2 * NZ + zz) * SPAN, SPAN)
                seq[pl.ds(at, SPAN), :] = pieces[last][row, :]
    seq[pl.ds(TOTAL, TILE), :] = jnp.zeros((TILE, HD), bf16)


def prepare_kernel(q_hbm, o_hbm, g_hbm, qs, gs, qt, gt, delta, q_ref, o_ref, g_ref, sems):
    copies = [
        pltpu.make_async_copy(s, d, sems.at[i])
        for i, (s, d) in enumerate(((q_hbm, q_ref), (o_hbm, o_ref), (g_hbm, g_ref)))
    ]
    for c in copies:
        c.start()
    for c in copies:
        c.wait()
    for a in range(2):
        prods = []
        for h in range(GROUP):
            dst = pl.ds(a * ROWS + h * SPAN, SPAN)
            src = (pl.ds(a * SPAN, SPAN), pl.ds(h * HD, HD))
            qs[dst, :] = q_ref[src]
            gs[dst, :] = g_ref[src]
            prods.append(g_ref[src].astype(f32) * o_ref[src].astype(f32))
        rows = pl.ds(a * ROWS, ROWS)
        qt[:, rows] = qs[rows, :].T
        gt[:, rows] = gs[rows, :].T
        prod = jnp.concatenate(prods, axis=0)
        high = prod.astype(bf16)
        low = (prod - high.astype(f32)).astype(bf16)
        ones = jnp.ones((16, HD), bf16)
        delta[pl.ds(a * 8, 8), :] = (nt(ones, high) + nt(ones, low))[:8]


def score_kernel(
    meta_ref, qt, k0, k1, k2, k3, weights0, weights1, peaks_ref, top_ref, kseq, peak, mass
):
    sorted_blocks(meta_ref, (k0, k1, k2, k3), kseq, True)

    def span(a, rows, tiles):
        peak[...] = jnp.full_like(peak, NEG)
        mass[...] = jnp.zeros_like(mass)

        weights, peaks = (weights0, weights1)[a], peaks_ref.at[a]

        def stats(t, at, pick):
            k = kseq[pl.ds(at, TILE), :]
            for c in range(0, ROWS, 256):
                cols = pl.ds(c, 256)
                s = pick(nn(k, qt[:, pl.ds(a * ROWS + c, 256)]), NEG, c, 256)
                old = peak[:, cols]
                fresh = jnp.maximum(old, jnp.max(s, axis=0, keepdims=True))
                e = jnp.exp2(s * (SCALE * LOG2E) - fresh * (SCALE * LOG2E))
                mass[:, cols] = mass[:, cols] * jnp.exp2((old - fresh) * (SCALE * LOG2E)) + jnp.sum(
                    e, axis=0, keepdims=True
                )
                peak[:, cols] = fresh
                peaks[t, :, cols] = jnp.broadcast_to(fresh, (8, 256))
                weights[t, :, cols] = e

        tiles(stats)
        top_ref[pl.ds(a * 8, 4), :] = jnp.broadcast_to(peak[...], (4, ROWS))
        top_ref[pl.ds(a * 8 + 4, 4), :] = jnp.broadcast_to(mass[...], (4, ROWS))

    each_query_span(meta_ref, span)


def key_value_kernel(
    meta_ref, qs, gs, gt, delta_ref, top_ref, weights0, weights1, peaks_ref, v0, v1, v2, v3,
    dkv_hbm, lse_ref, vseq, acc, out, sems,
):
    sorted_blocks(meta_ref, (v0, v1, v2, v3), vseq, False)
    acc[...] = jnp.zeros_like(acc)

    def span(a, rows, tiles):
        high, mass = top_ref[pl.ds(a * 8, 1), :], top_ref[pl.ds(a * 8 + 4, 1), :]
        lse = high * (SCALE * LOG2E) + jnp.log2(mass)
        lse_ref[pl.ds(a * 8, 8), :] = jnp.broadcast_to(lse, (8, ROWS))
        inverse = 1.0 / mass
        delta = delta_ref[pl.ds(a * 8, 1), :]

        weights, peaks = (weights0, weights1)[a], peaks_ref.at[a]

        def step(t, at, pick):
            v = vseq[pl.ds(at, TILE), :]
            dk, dv = acc[pl.ds(at, TILE), :HD], acc[pl.ds(at, TILE), HD:]
            for c in range(0, ROWS, 256):
                cols, some = pl.ds(c, 256), pl.ds(a * ROWS + c, 256)
                w = jnp.exp2((peaks[t, :, cols][:1] - high[:, c : c + 256]) * (SCALE * LOG2E)) * inverse[:, c : c + 256]
                p = weights[t, :, cols] * w
                ds = p * (nn(v, gt[:, some]) - delta[:, c : c + 256])
                dv = dv + nn(p.astype(bf16), gs[some, :])
                dk = dk + nn(ds.astype(bf16), qs[some, :])
            acc[pl.ds(at, TILE), :HD] = dk
            acc[pl.ds(at, TILE), HD:] = dv

        tiles(step, masked=False)

    each_query_span(meta_ref, span)
    copies = []
    for part in range(PARTS):
        for slot in range(part * SPANS // PARTS, (part + 1) * SPANS // PARTS):
            at = slot_place(meta_ref, slot)
            row = pl.ds(slot * SPAN, SPAN)
            out[row, :HD] = (acc[pl.ds(at, SPAN), :HD] * SCALE).astype(bf16)
            out[row, HD:] = acc[pl.ds(at, SPAN), HD:].astype(bf16)
        rows = pl.ds(part * TOTAL // PARTS, TOTAL // PARTS)
        copies.append(pltpu.make_async_copy(out.at[rows], dkv_hbm.at[rows], sems.at[part]))
        copies[-1].start()
    for c in copies:
        c.wait()


def query_kernel(
    meta_ref, qt, gt, delta_ref, lse_ref, k0, k1, k2, k3, v0, v1, v2, v3,
    dq_ref, sq_ref, kseq, vseq, acc,
):
    sorted_blocks(meta_ref, (k0, k1, k2, k3), kseq, True)
    sorted_blocks(meta_ref, (v0, v1, v2, v3), vseq, False)
    square = []

    def span(a, rows, tiles):
        lse, delta = lse_ref[pl.ds(a * 8, 1), :], delta_ref[pl.ds(a * 8, 1), :]
        acc[...] = jnp.zeros_like(acc)

        def step(t, at, pick):
            k = kseq[pl.ds(at, TILE), :]
            p = pick(jnp.exp2(nn(k, qt[:, rows]) * (SCALE * LOG2E) - lse), 0.0)
            ds = p * (nn(vseq[pl.ds(at, TILE), :], gt[:, rows]) - delta)
            acc[...] += tn(k, ds.astype(bf16))

        tiles(step)
        dq = (acc[...] * SCALE).T.astype(bf16)
        for h in range(GROUP):
            dq_ref[pl.ds(a * SPAN, SPAN), pl.ds(h * HD, HD)] = dq[h * SPAN : (h + 1) * SPAN]
        dq = dq.astype(f32)
        square.append(jnp.sum(jnp.sum(dq * dq, axis=0, keepdims=True), axis=1, keepdims=True))

    each_query_span(meta_ref, span)
    sq_ref[...] = jnp.broadcast_to(square[0] + square[1], sq_ref.shape)


def half_sum(parts_ref, index):
    total = parts_ref[0, index].astype(f32)
    for h in range(1, NY * NX):
        total = total + parts_ref[h, index].astype(f32)
    return total


def other_kernel(parts_ref, other_ref):
    other_ref[...] = half_sum(parts_ref, 1 - lax.axis_index("zh")).astype(bf16)


def own_kernel(parts_ref, own_ref):
    own_ref[...] = half_sum(parts_ref, lax.axis_index("zh"))


def finish_kernel(own_ref, other_ref, sq_ref, dk_ref, dv_ref, local_ref):
    total = own_ref[...]
    both = (total + other_ref[...].astype(f32)).astype(bf16)
    dk_ref[...] = both[:, :HD]
    dv_ref[...] = both[:, HD:]
    wide = both.astype(f32)
    local = jnp.sum(jnp.sum(wide * wide, axis=0, keepdims=True), axis=1, keepdims=True)
    local_ref[...] = jnp.broadcast_to((local + sq_ref[:1, :1])[None], local_ref.shape)


def call(kernel, outs, specs, scratch, flops, limit, *args):
    kind = {
        "S": pl.BlockSpec(memory_space=pltpu.SMEM),
        "H": pl.BlockSpec(memory_space=pl.ANY),
        "V": pl.BlockSpec(memory_space=pltpu.VMEM),
    }
    given, made = specs.split()
    args = [
        pltpu.with_memory_space_constraint(a, pltpu.HBM) if c == "H" else a
        for a, c in zip(args, given, strict=True)
    ]
    return pl.pallas_call(
        kernel,
        out_shape=tuple(
            pltpu.HBM(s, t) if c == "H" else jax.ShapeDtypeStruct(s, t)
            for (s, t), c in zip(outs, made, strict=True)
        ),
        in_specs=[kind[c] for c in given],
        out_specs=tuple(kind[c] for c in made),
        scratch_shapes=[
            pltpu.SemaphoreType.DMA(s) if t is None else pltpu.VMEM(s, t) for s, t in scratch
        ],
        compiler_params=pltpu.CompilerParams(vmem_limit_bytes=limit << 20),
        cost_estimate=pl.CostEstimate(flops=flops, bytes_accessed=4 << 20, transcendentals=0),
    )(*args)


def shift(a, axis, step):
    n = lax.axis_size(axis)
    return lax.ppermute(a, axis, [(i, (i + step) % n) for i in range(n)])


def shards(queries, keys, values, outputs, out_grad, doc_lengths, span_perm):
    tq = queries.shape[0]
    meta = jnp.concatenate([span_perm, doc_lengths])
    kv = jnp.stack([keys, values])
    kv = jnp.stack([kv, shift(kv, "zh", 1)], axis=1)
    k, v = kv[0], kv[1]
    k = [k] + [shift(k, "y", s) for s in range(1, NY)]
    v = [v] + [shift(v, "x", s) for s in range(1, NX)]
    mine = (queries.shape, bf16)
    heads, turned = ((2 * ROWS, HD), bf16), ((HD, 2 * ROWS), bf16)
    row, one, longer = ((16, ROWS), f32), ((1, ROWS), f32), ((TOTAL + TILE, HD), bf16)
    most = -(-(TOTAL // 2 + SPAN) // TILE)
    ready = call(
        prepare_kernel,
        [heads, heads, turned, turned, row],
        "HHH VVVVV",
        [mine, mine, mine, ((3,), None)],
        1 << 30, 16, queries, outputs, out_grad,
    )
    k, v, meta = lax.optimization_barrier((k, v, meta))
    qs, gs, qt, gt, delta = ready
    k, v = jnp.stack(k), jnp.stack(v)
    k = [k] + [shift(k, "x", s) for s in range(1, NX)]
    v = [v] + [shift(v, "y", s) for s in range(1, NY)]
    k = [a.reshape(TOTAL // NY, HD) for a in k]
    v = [a.reshape(TOTAL // NX, HD) for a in v]

    weights0, weights1, peaks, top = call(
        score_kernel,
        [((most, TILE, ROWS), f32), ((most, TILE, ROWS), f32), ((2, most, 8, ROWS), f32), row],
        "SVVVVV VVVV",
        [longer, one, one],
        8 << 30, 16, meta, qt, *k,
    )
    parts, lse = call(
        key_value_kernel,
        [((TOTAL, 2 * HD), bf16), row],
        "SVVVVVVVVVVVV HV",
        [longer, ((TOTAL + TILE, 2 * HD), f32), ((TOTAL, 2 * HD), bf16), ((PARTS,), None)],
        16 << 30, 16, meta, qs, gs, gt, delta, top, weights0, weights1, peaks, *v,
    )
    parts = parts.reshape(NY * NX, NZ, tq, 2 * HD)
    parts = lax.all_to_all(parts, ("y", "x"), 0, 0)
    query_grad, square = call(
        query_kernel,
        [mine, ((8, HD), f32)],
        "SVVVVVVVVVVVV VV",
        [longer, longer, ((HD, ROWS), f32)],
        16 << 30, 32, meta, qt, gt, delta, lse, *k, *v,
    )
    parts, query_grad, square = lax.optimization_barrier((parts, query_grad, square))
    half = ((tq, HD), bf16)
    (other,) = call(other_kernel, [((tq, 2 * HD), bf16)], "V V", [], 1 << 20, 16, parts)
    (own,) = call(own_kernel, [((tq, 2 * HD), f32)], "V V", [], 1 << 30, 16, parts)
    every = ("y", "x", "zh", "tp")
    key_grad, value_grad, local = call(
        finish_kernel,
        [half, half, ((lax.axis_size(every), 1, HD), f32)],
        "VVV VVV",
        [], 1 << 20, 16, own, shift(other, "zh", 1), square,
    )
    grad_square = jnp.sum(lax.all_to_all(local, every, 0, 0)[:, 0, 0])
    return (query_grad, key_grad, value_grad, grad_square)


def solution(mesh):
    tp = mesh.devices.shape[1]
    split = Mesh(mesh.devices.reshape(NY, NX, NZ, tp), ("y", "x", "zh", "tp"))
    both = P(("y", "x", "zh"), "tp")
    return jax.shard_map(
        shards,
        mesh=split,
        in_specs=(both,) * 5 + (P(), P()),
        out_specs=(both, both, both, P()),
        check_vma=False,
    )
```
